32 devices in a mesh: col: 8 (over z, x), sub: 4 (over y, core).
Axes of the slice: x: 2, y: 2, z: 4, core: 2. Of those that a mesh axis runs over, the one named last changes fastest.
Arguments:
- right_sides: float32 [16, 16384], P(None, ('col', 'sub')), may hold values from -40 to 40
- left_bases: bfloat16 [16384, 2048], P(('col', 'sub')), may hold values from -0.25 to 0.25
- right_bases: bfloat16 [32, 64, 16384], P(None, None, ('col', 'sub')), may hold values from -0.25 to 0.25
- tile_scales: float32 [32, 32, 64], P(None, ('col', 'sub')), may hold values from 0.002 to 0.03
- tile_ranks: int32 [32, 32], P(None, ('col', 'sub')), may hold values from 8 to 64, as said below
- near_field: bfloat16 [16384, 512], P(('col', 'sub')), may hold values from -0.078125 to 0.078125
- diagonal: float32 [16384], P(('col', 'sub')), may hold values from 1 to 3
Outputs:
- solution: float32 [16, 16384], P(None, ('col', 'sub'))
- residual: float32 [16, 16384], P(None, ('col', 'sub'))
The draws below stay inside these ranges and needn't reach their ends.
Inputs may be any that keep to these rules, and one draw needn't show every extreme that they name: Tile (i, j) uses the first tile_ranks[i, j] columns of its bases; every diagonal tile uses all 64.
All inputs are finite; a program needn't handle non-finite values.
Results may differ from the reference program's by a relative error of at most 0.006.
Values may be sent and summed in bfloat16 or wider, within the bound.
A program may use at most 128 MiB of HBM per device.

```python
import math
import jax
import jax.numpy as jnp
from jax import lax

TILE = 512
RANK = 64
NRHS = 16
ITERS = 2
NT = 32
ORDER = 16384


def draw_right_sides(key, part):
    key = jax.random.fold_in(key, 11)
    key_base, key_rows, key_cols = jax.random.split(key, 3)
    row_scale = jnp.exp(jax.random.uniform(key_rows, (NRHS, 1), jnp.float32, 0.0, math.log(10.0)))
    col_scale = jnp.exp(jax.random.uniform(key_cols, (1, ORDER), jnp.float32, 0.0, math.log(10.0)))
    base = jnp.clip(jax.random.normal(key_base, (NRHS, ORDER), jnp.float32), -4.0, 4.0)
    return 0.1 * base * row_scale * col_scale


def draw_tile_ranks(key, part):
    key = jax.random.fold_in(key, 23)
    drawn = jax.random.randint(key, (NT, NT), RANK // 8, RANK + 1, jnp.int32)
    on_diagonal = lax.broadcasted_iota(jnp.int32, (NT, NT), 0) == lax.broadcasted_iota(jnp.int32, (NT, NT), 1)
    return jnp.where(on_diagonal, jnp.full((NT, NT), RANK, jnp.int32), drawn)


def block_scale(stream_key, dims, shards, least, largest):
    def one(axis_at, parts):
        heights = jax.random.uniform(jax.random.fold_in(jax.random.fold_in(stream_key, 6), axis_at), (parts,), jnp.float32, least / len(shards), largest / len(shards))
        return jnp.repeat(jnp.exp(heights), dims[axis_at] // parts).reshape((-1,) + (1,) * (len(dims) - axis_at - 1))

    level = one(*shards[0])
    for cut in shards[1:]:
        level = level * one(*cut)
    return level


def gaussian(stream_key, shape, width, most, pieces=(), kind=jnp.bfloat16):
    array = width * jax.random.normal(stream_key, shape, jnp.float32)
    if pieces:
        array = array * block_scale(stream_key, shape, pieces, -0.22, 0.18)
    return jnp.clip(array, -most, most).astype(kind)


def setup_inputs(seed: int = 0) -> dict:
    keys = jax.random.split(jax.random.key(seed), 8)
    return {
        "right_sides": draw_right_sides(jax.random.fold_in(keys[7], 71), 0),
        "left_bases": gaussian(keys[1], (ORDER, NT * RANK), TILE ** -0.5, 0.25, ((0, 32),)),
        "right_bases": gaussian(keys[2], (NT, RANK, ORDER), TILE ** -0.5, 0.25, ((2, 32),)),
        "tile_scales": jnp.clip(jnp.exp(math.log(0.03) - 2.70805 * jax.random.uniform(keys[3], (NT, NT, RANK), jnp.float32) ** block_scale(keys[3], (NT, NT, RANK), ((1, 32),), -0.2, 0.2)), 0.002, 0.03),
        "tile_ranks": draw_tile_ranks(jax.random.fold_in(keys[7], 71), 0),
        "near_field": gaussian(keys[5], (ORDER, TILE), (11 * TILE) ** -0.5, 0.078125, ((0, 32),)),
        "diagonal": jnp.clip(1.0 + 2.0 * jax.random.uniform(keys[6], (ORDER,), jnp.float32) ** block_scale(keys[6], (ORDER,), ((0, 32),), -0.2, 0.2), 1.0, 3.0),
    }


highest = lax.Precision.HIGHEST

def gram_of(first_rows, second_rows):
    return jnp.dot(first_rows, second_rows.T, precision=highest)

def apply_matrix(vectors, left_bases, right_bases, weights, near_field, diagonal):
    rounded = lax.optimization_barrier(vectors.astype(jnp.bfloat16)).astype(jnp.float32)
    rounded = rounded.reshape(NRHS, NT, TILE)

    def row_terms(operands):
        bases_row, weight_row = operands
        product = jnp.einsum('rjt,njt->jnr', bases_row.astype(jnp.float32).reshape(RANK, NT, TILE), rounded)
        return (product * weight_row[:, None, :]).astype(jnp.bfloat16)
    coefficients = lax.map(row_terms, (right_bases, weights))

    def row_output(operands):
        left_row, coeff_row = operands
        return jnp.einsum('pjr,jnr->np', left_row.astype(jnp.float32).reshape(TILE, NT, RANK), coeff_row.astype(jnp.float32))
    far_term = lax.map(row_output, (left_bases.reshape(NT, TILE, NT * RANK), coefficients))
    near_term = jnp.einsum('ipq,niq->nip', near_field.astype(jnp.float32).reshape(NT, TILE, TILE), rounded)
    far_flat = jnp.transpose(far_term, (1, 0, 2)).reshape(NRHS, ORDER)
    return diagonal[None, :] * vectors + near_term.reshape(NRHS, ORDER) + far_flat

def reference(right_sides, left_bases, right_bases, tile_scales, tile_ranks, near_field, diagonal):
    keep_mask = jnp.arange(RANK, dtype=jnp.int32)[None, None, :] < tile_ranks[:, :, None]
    weights = jnp.where(keep_mask, tile_scales, jnp.zeros_like(tile_scales))

    def apply_now(vectors):
        return apply_matrix(vectors, left_bases, right_bases, weights, near_field, diagonal)
    start_factor = jnp.linalg.cholesky(gram_of(right_sides, right_sides))
    basis_list = [jax.scipy.linalg.solve_triangular(start_factor, right_sides, lower=True)]
    hess_rows = []
    for iteration in range(ITERS):
        next_vectors = apply_now(basis_list[iteration])
        stacked = jnp.concatenate(basis_list, axis=0)
        projections = gram_of(next_vectors, stacked)
        next_vectors = next_vectors - jnp.dot(projections, stacked, precision=highest)
        factor_low = jnp.linalg.cholesky(gram_of(next_vectors, next_vectors))
        if iteration + 1 < ITERS:
            basis_list.append(jax.scipy.linalg.solve_triangular(factor_low, next_vectors, lower=True))
        padding = jnp.zeros((NRHS, NRHS * (ITERS - iteration - 1)), jnp.float32)
        hess_rows.append(jnp.concatenate([projections, factor_low, padding], axis=1))
    hessenberg = jnp.concatenate(hess_rows, axis=0)
    normal_matrix = jnp.dot(hessenberg, hessenberg.T, precision=highest)
    right_term = jnp.dot(start_factor, hessenberg[:, :NRHS].T, precision=highest)
    normal_factor = jnp.linalg.cholesky(normal_matrix)
    coordinates = jax.scipy.linalg.cho_solve((normal_factor, True), right_term.T).T
    solution = jnp.dot(coordinates, jnp.concatenate(basis_list, axis=0), precision=highest)
    residual = right_sides - apply_now(solution)
    return (solution, residual)
```

```python
import functools

import jax
import jax.numpy as jnp
from jax import lax
from jax.experimental import pallas as pl
from jax.experimental.pallas import tpu as pltpu
from jax.sharding import PartitionSpec as P

MESH = pl.DeviceIdType.MESH
SHIFT = 2.0
highest = lax.Precision.HIGHEST


def dot_rows(first, second, precision=None):
    return lax.dot_general(
        first, second, (((1,), (1,)), ((), ())),
        preferred_element_type=jnp.float32, precision=precision,
    )


def split_rows(values):
    high = values.astype(jnp.bfloat16)
    low = (values - high.astype(jnp.float32)).astype(jnp.bfloat16)
    return jnp.concatenate([high, low], axis=0)


def join_rows(product):
    half = product.shape[0] // 2
    return product[:half] + product[half:]


def kernel(
    sub_count, tiles, chunk,
    rhs_ref, scales_ref, ranks_ref, diag_ref, right_hbm, left_hbm, near_hbm,
    sol_ref, res_ref,
    right, left, near, coeff_out, coeff_in, gram_out, gram_in, gathered,
    load_sem, send_sem, recv_sem,
):
    me = lax.axis_index("col") * sub_count + lax.axis_index("sub")
    chunks = right.shape[0] // chunk
    right_loads = []
    for c in range(chunks):
        rows = pl.ds(c * chunk, chunk)
        right_loads.append(
            pltpu.make_async_copy(right_hbm.at[rows], right.at[rows], load_sem.at[c])
        )
    near_load = pltpu.make_async_copy(near_hbm, near, load_sem.at[chunks])
    left_load = pltpu.make_async_copy(left_hbm, left, load_sem.at[chunks + 1])
    for load in right_loads:
        load.start()
    near_load.start()
    left_load.start()

    barrier = pltpu.get_barrier_semaphore()

    def partner(step):
        other = lax.rem(me + step, tiles)
        return other, (other // sub_count, lax.rem(other, sub_count))

    def greet(step, carry):
        pl.semaphore_signal(barrier, inc=1, device_id=partner(step)[1], device_id_type=MESH)
        return carry

    lax.fori_loop(1, tiles, greet, 0)

    lane = lax.broadcasted_iota(jnp.int32, (8, 128), 1)
    in_first = lane < 64

    def swap(block):
        return pltpu.roll(block, 64, 1)

    ranks = ranks_ref[...]
    keep = lax.broadcasted_iota(jnp.int32, scales_ref.shape, 1) < ranks
    weights = jnp.where(keep, scales_ref[...], 0.0)

    def project(stacked, phase, first):
        for c in range(chunks):
            if first:
                right_loads[c].wait()
            product = join_rows(dot_rows(stacked, right[pl.ds(c * chunk, chunk)]))
            for m in range(chunk // 128):
                i = c * (chunk // 64) + 2 * m
                pair = product[:, m * 128:(m + 1) * 128]
                pair = pair * jnp.concatenate([weights[i:i + 1], weights[i + 1:i + 2]], axis=1)
                upper, lower = pair[:8], pair[8:]
                coeff_out[phase, i] = jnp.where(in_first, upper, swap(lower))
                coeff_out[phase, i + 1] = jnp.where(in_first, swap(upper), lower)

    def send_coefficients(phase):
        def send(step, carry):
            other, where = partner(step)
            pltpu.make_async_remote_copy(
                src_ref=coeff_out.at[phase, other],
                dst_ref=coeff_in.at[phase, me],
                send_sem=send_sem.at[phase],
                recv_sem=recv_sem.at[phase],
                device_id=where,
                device_id_type=MESH,
            ).start()
            return carry

        lax.fori_loop(1, tiles, send, 0)
        coeff_in[phase, me] = coeff_out[phase, me]

    def send_gram(which):
        def send(step, carry):
            where = partner(step)[1]
            pltpu.make_async_remote_copy(
                src_ref=gram_out.at[which],
                dst_ref=gram_in.at[which, me],
                send_sem=send_sem.at[2 + which],
                recv_sem=recv_sem.at[2 + which],
                device_id=where,
                device_id_type=MESH,
            ).start()
            return carry

        lax.fori_loop(1, tiles, send, 0)
        gram_in[which, me] = gram_out[which]

    def all_of(buffer, index, slot):
        blocks = buffer.at[index, pl.ds(0, tiles - 1)]
        return pltpu.make_async_remote_copy(
            src_ref=blocks, dst_ref=blocks, send_sem=send_sem.at[slot], recv_sem=recv_sem.at[slot],
            device_id=partner(1)[1], device_id_type=MESH,
        )

    def far_field(phase):
        for m in range(tiles // 2):
            even, odd = coeff_in[phase, 2 * m], coeff_in[phase, 2 * m + 1]
            upper = jnp.where(in_first, even, swap(odd))
            lower = jnp.where(in_first, swap(even), odd)
            gathered[:, m * 128:(m + 1) * 128] = split_rows(jnp.concatenate([upper, lower], axis=0))
        return join_rows(dot_rows(gathered[...], left[...]))

    rhs = rhs_ref[...]
    diag = diag_ref[...]
    stacked = split_rows(rhs)
    project(stacked, 0, True)
    pl.semaphore_wait(barrier, tiles - 1)
    send_coefficients(0)
    near_load.wait()
    moved = (diag - SHIFT) * rhs + join_rows(dot_rows(stacked, near[...]))
    left_load.wait()
    all_of(coeff_in, 0, 0).wait_recv()
    moved = moved + far_field(0)
    image_1 = moved + SHIFT * rhs

    stacked = split_rows(moved)
    project(stacked, 1, False)
    send_coefficients(1)
    early = dot_rows(image_1, jnp.concatenate([rhs, image_1], axis=0), highest)
    early = jnp.concatenate([early, jnp.zeros_like(early)], axis=1)
    gram_out[0] = jnp.concatenate([early[:8], early[8:]], axis=1)
    send_gram(0)
    image_2 = diag * moved + join_rows(dot_rows(stacked, near[...]))
    all_of(coeff_in, 1, 1).wait_recv()
    image_2 = image_2 + far_field(1)

    late = dot_rows(image_2, jnp.concatenate([rhs, image_1, image_2], axis=0), highest)
    cross = dot_rows(image_1, image_2, highest)
    late = jnp.concatenate([late, cross], axis=1)
    gram_out[1] = jnp.concatenate([late[:8], late[8:]], axis=1)
    send_gram(1)

    def total(which):
        all_of(gram_in, which, 2 + which).wait_recv()
        summed = jnp.sum(gram_in[which], axis=0)
        return jnp.concatenate([summed, swap(summed)], axis=0)

    early = total(0)
    late = total(1)
    top = jnp.where(
        lax.broadcasted_iota(jnp.int32, early.shape, 1) < 32, early, pltpu.roll(late, 112, 1)
    )
    system = jnp.concatenate([top, late], axis=0)
    row_at = lax.broadcasted_iota(jnp.int32, system.shape, 0)
    for k in range(32):
        pivot = system[k:k + 1, 16 + k:17 + k]
        scaled = system[k:k + 1] * (1.0 / pivot)
        system = jnp.where(row_at == k, scaled, system - system[:, 16 + k:17 + k] * scaled)
    weights_out = jnp.transpose(system)[:16, :32]

    sol_ref[...] = jnp.dot(weights_out, jnp.concatenate([rhs, moved], axis=0), precision=highest)
    res_ref[...] = rhs - jnp.dot(
        weights_out, jnp.concatenate([image_1, image_2], axis=0), precision=highest
    )
    all_of(coeff_in, 0, 0).wait_send()
    all_of(coeff_in, 1, 1).wait_send()
    all_of(gram_in, 0, 2).wait_send()
    all_of(gram_in, 1, 3).wait_send()


def on_device(
    sub_count, right_sides, left_bases, right_bases, tile_scales, tile_ranks, near_field, diagonal
):
    rhs_count, cells = right_sides.shape
    tiles, rank_len, _ = right_bases.shape
    features = tiles * rank_len
    chunk = min(512, features)
    vmem = pl.BlockSpec(memory_space=pltpu.VMEM)
    anywhere = pl.BlockSpec(memory_space=pl.ANY)
    return pl.pallas_call(
        functools.partial(kernel, sub_count, tiles, chunk),
        out_shape=[jax.ShapeDtypeStruct((rhs_count, cells), jnp.float32)] * 2,
        in_specs=[vmem] * 4 + [anywhere] * 3,
        out_specs=[vmem] * 2,
        scratch_shapes=[
            pltpu.VMEM((features, cells), jnp.bfloat16),
            pltpu.VMEM((cells, features), jnp.bfloat16),
            pltpu.VMEM((cells, cells), jnp.bfloat16),
            pltpu.VMEM((2, tiles, 8, 128), jnp.float32),
            pltpu.VMEM((2, tiles, 8, 128), jnp.float32),
            pltpu.VMEM((2, 8, 128), jnp.float32),
            pltpu.VMEM((2, tiles, 8, 128), jnp.float32),
            pltpu.VMEM((2 * rhs_count, features), jnp.bfloat16),
            pltpu.SemaphoreType.DMA((features // chunk + 2,)),
            pltpu.SemaphoreType.DMA((4,)),
            pltpu.SemaphoreType.DMA((4,)),
        ],
        compiler_params=pltpu.CompilerParams(
            collective_id=0, has_side_effects=True, vmem_limit_bytes=48 * 1024 * 1024
        ),
    )(
        right_sides,
        tile_scales.reshape(tiles, rank_len),
        tile_ranks,
        diagonal.reshape(1, cells),
        right_bases.reshape(features, cells),
        left_bases,
        near_field,
    )


def solution(mesh):
    both = ("col", "sub")
    in_specs = (
        P(None, both), P(both, None), P(None, None, both), P(None, both, None),
        P(None, both), P(both, None), P(both),
    )
    return jax.shard_map(
        functools.partial(on_device, mesh.shape["sub"]), mesh=mesh, in_specs=in_specs,
        out_specs=(P(None, both), P(None, both)), check_vma=False,
    )
```

```python
import functools

import jax
import jax.numpy as jnp
from jax import lax
from jax.experimental import pallas as pl
from jax.experimental.pallas import tpu as pltpu
from jax.sharding import PartitionSpec as P

MESH = pl.DeviceIdType.MESH
SHIFT = 2.0
PIVOTS = 8
VMEM_BYTES = 60 * 1024 * 1024
highest = lax.Precision.HIGHEST


def dot_rows(first, second, precision=None):
    return lax.dot_general(
        first, second, (((1,), (1,)), ((), ())),
        preferred_element_type=jnp.float32, precision=precision,
    )


def split_rows(values):
    high = values.astype(jnp.bfloat16)
    low = (values - high.astype(jnp.float32)).astype(jnp.bfloat16)
    return jnp.concatenate([high, low], axis=0)


def join_rows(product):
    half = product.shape[0] // 2
    return product[:half] + product[half:]


def kernel(
    col_count, sub_count, tiles, chunk,
    rhs_hbm, scales_hbm, ranks_hbm, diag_hbm, right_hbm, left_hbm, near_hbm,
    sol_ref, res_ref,
    rhs_ref, scales_ref, ranks_ref, diag_ref, right, left, near,
    coeff_out, coeff_in, gram_out, gram_near, gram_far, gathered,
    load_sem, send_sem, recv_sem,
):
    my_col, my_sub = lax.axis_index("col"), lax.axis_index("sub")
    me = my_col * sub_count + my_sub
    chunks = right.shape[0] // chunk
    small_loads = [
        pltpu.make_async_copy(source, target, load_sem.at[chunks + 2 + n])
        for n, (source, target) in enumerate([
            (rhs_hbm, rhs_ref), (scales_hbm, scales_ref),
            (ranks_hbm, ranks_ref), (diag_hbm, diag_ref),
        ])
    ]
    right_loads = []
    for c in range(chunks):
        rows = pl.ds(c * chunk, chunk)
        right_loads.append(
            pltpu.make_async_copy(right_hbm.at[rows], right.at[rows], load_sem.at[c])
        )
    near_load = pltpu.make_async_copy(near_hbm, near, load_sem.at[chunks])
    left_load = pltpu.make_async_copy(left_hbm, left, load_sem.at[chunks + 1])
    for load in small_loads + right_loads:
        load.start()
    near_load.start()
    left_load.start()

    barrier = pltpu.get_barrier_semaphore()
    subs = [my_sub] + [lax.rem(my_sub + step, sub_count) for step in range(1, sub_count)]

    def each_partner(act):
        for sub in subs[1:]:
            act(my_col, sub)

        def column(step, carry):
            col = lax.rem(my_col + step, col_count)
            for sub in subs:
                act(col, sub)
            return carry

        lax.fori_loop(1, col_count, column, 0)

    def greet(col, sub):
        pl.semaphore_signal(barrier, inc=1, device_id=(col, sub), device_id_type=MESH)

    each_partner(greet)

    lane = lax.broadcasted_iota(jnp.int32, (8, 128), 1)
    in_first = lane < 64

    def swap(block):
        return pltpu.roll(block, 64, 1)

    for load in small_loads:
        load.wait()
    square = (tiles, tiles)
    on_diagonal = lax.broadcasted_iota(jnp.int32, square, 0) == lax.broadcasted_iota(
        jnp.int32, square, 1
    )
    ranks = jnp.sum(jnp.where(on_diagonal, ranks_ref[...], 0), axis=1, keepdims=True)
    keep = lax.broadcasted_iota(jnp.int32, scales_ref.shape, 1) < ranks
    weights = jnp.where(keep, scales_ref[...], 0.0)

    def project(stacked, phase, first):
        for c in range(chunks):
            if first:
                right_loads[c].wait()
            product = join_rows(dot_rows(stacked, right[pl.ds(c * chunk, chunk)]))
            for m in range(chunk // 128):
                i = c * (chunk // 64) + 2 * m
                pair = product[:, m * 128:(m + 1) * 128]
                pair = pair * jnp.concatenate([weights[i:i + 1], weights[i + 1:i + 2]], axis=1)
                upper, lower = pair[:8], pair[8:]
                coeff_out[phase, i] = jnp.where(in_first, upper, swap(lower))
                coeff_out[phase, i + 1] = jnp.where(in_first, swap(upper), lower)

    def remote(source, target, slot, col, sub):
        return pltpu.make_async_remote_copy(
            src_ref=source, dst_ref=target, send_sem=send_sem.at[slot], recv_sem=recv_sem.at[slot],
            device_id=(col, sub), device_id_type=MESH,
        )

    def send_coefficients(phase):
        def send(col, sub):
            other = col * sub_count + sub
            remote(coeff_out.at[phase, other], coeff_in.at[phase, me], phase, col, sub).start()

        each_partner(send)
        coeff_in[phase, me] = coeff_out[phase, me]

    def all_of(blocks, slot):
        return remote(blocks, blocks, slot, my_col, subs[1])

    def coefficients_of(phase):
        return all_of(coeff_in.at[phase, pl.ds(0, tiles - 1)], phase)

    near_grams = all_of(gram_near.at[pl.ds(0, sub_count - 1)], 2)
    far_grams = all_of(gram_far.at[pl.ds(0, col_count - 1)], 3)

    def far_field(phase):
        for m in range(tiles // 2):
            even, odd = coeff_in[phase, 2 * m], coeff_in[phase, 2 * m + 1]
            upper = jnp.where(in_first, even, swap(odd))
            lower = jnp.where(in_first, swap(even), odd)
            gathered[:, m * 128:(m + 1) * 128] = split_rows(jnp.concatenate([upper, lower], axis=0))
        return join_rows(dot_rows(gathered[...], left[...]))

    rhs = rhs_ref[...]
    diag = diag_ref[...]
    stacked = split_rows(rhs)
    project(stacked, 0, True)
    pl.semaphore_wait(barrier, tiles - 1)
    send_coefficients(0)
    near_load.wait()
    moved = (diag - SHIFT) * rhs + join_rows(dot_rows(stacked, near[...]))
    left_load.wait()
    coefficients_of(0).wait_recv()
    moved = moved + far_field(0)
    image_1 = moved + SHIFT * rhs

    stacked = split_rows(moved)
    project(stacked, 1, False)
    send_coefficients(1)
    early = dot_rows(image_1, jnp.concatenate([rhs, image_1], axis=0), highest)
    early = jnp.concatenate([early, jnp.zeros_like(early)], axis=1)
    gram_out[0, :8] = jnp.concatenate([early[:8], early[8:]], axis=1)
    image_2 = diag * moved + join_rows(dot_rows(stacked, near[...]))
    coefficients_of(1).wait_recv()
    image_2 = image_2 + far_field(1)

    late = dot_rows(image_2, jnp.concatenate([rhs, image_1, image_2], axis=0), highest)
    cross = dot_rows(image_1, image_2, highest)
    late = jnp.concatenate([late, cross], axis=1)
    gram_out[0, 8:] = jnp.concatenate([late[:8], late[8:]], axis=1)

    for sub in subs[1:]:
        remote(gram_out.at[0], gram_near.at[my_sub], 2, my_col, sub).start()
    gram_near[my_sub] = gram_out[0]
    near_grams.wait_recv()
    gram_out[1] = jnp.sum(gram_near[...], axis=0)
    for step in range(1, col_count):
        col = lax.rem(my_col + step, col_count)
        remote(gram_out.at[1], gram_far.at[my_col], 3, col, my_sub).start()
    gram_far[my_col] = gram_out[1]
    far_grams.wait_recv()
    summed = jnp.sum(gram_far[...], axis=0)

    def unfold(block):
        return jnp.concatenate([block, swap(block)], axis=0)

    early, late = unfold(summed[:8]), unfold(summed[8:])
    top = jnp.where(
        lax.broadcasted_iota(jnp.int32, early.shape, 1) < 32, early, pltpu.roll(late, 112, 1)
    )
    system = jnp.concatenate([top, late], axis=0)
    row_at = lax.broadcasted_iota(jnp.int32, system.shape, 0)
    for start in range(0, 32, PIVOTS):
        columns = [
            jnp.broadcast_to(system[:, 16 + k:17 + k], system.shape)
            for k in range(start, start + PIVOTS)
        ]
        for n in range(PIVOTS):
            k = start + n
            factors = columns[n]
            inverse = 1.0 / factors[k:k + 1]

            def eliminate(block):
                scaled = block[k:k + 1] * inverse
                return jnp.where(row_at == k, scaled, block - factors * scaled)

            columns[n + 1:] = [eliminate(column) for column in columns[n + 1:]]
            system = eliminate(system)
    weights_out = jnp.transpose(system)[:16, :32]

    sol_ref[...] = jnp.dot(weights_out, jnp.concatenate([rhs, moved], axis=0), precision=highest)
    res_ref[...] = rhs - jnp.dot(
        weights_out, jnp.concatenate([image_1, image_2], axis=0), precision=highest
    )
    coefficients_of(0).wait_send()
    coefficients_of(1).wait_send()
    near_grams.wait_send()
    far_grams.wait_send()


def on_device(
    col_count, sub_count, right_sides, left_bases, right_bases, tile_scales, tile_ranks, near_field,
    diagonal,
):
    rhs_count, cells = right_sides.shape
    tiles, rank_len, _ = right_bases.shape
    features = tiles * rank_len
    chunk = min(512, features)
    vmem = pl.BlockSpec(memory_space=pltpu.VMEM)
    anywhere = pl.BlockSpec(memory_space=pl.ANY)
    return pl.pallas_call(
        functools.partial(kernel, col_count, sub_count, tiles, chunk),
        out_shape=[jax.ShapeDtypeStruct((rhs_count, cells), jnp.float32)] * 2,
        in_specs=[anywhere] * 7,
        out_specs=[vmem] * 2,
        scratch_shapes=[
            pltpu.VMEM((rhs_count, cells), jnp.float32),
            pltpu.VMEM((tiles, rank_len), jnp.float32),
            pltpu.VMEM((1, tiles), jnp.int32),
            pltpu.VMEM((1, cells), jnp.float32),
            pltpu.VMEM((features, cells), jnp.bfloat16),
            pltpu.VMEM((cells, features), jnp.bfloat16),
            pltpu.VMEM((cells, cells), jnp.bfloat16),
            pltpu.VMEM((2, tiles, 8, 128), jnp.float32),
            pltpu.VMEM((2, tiles, 8, 128), jnp.float32),
            pltpu.VMEM((2, 16, 128), jnp.float32),
            pltpu.VMEM((sub_count, 16, 128), jnp.float32),
            pltpu.VMEM((col_count, 16, 128), jnp.float32),
            pltpu.VMEM((2 * rhs_count, features), jnp.bfloat16),
            pltpu.SemaphoreType.DMA((features // chunk + 6,)),
            pltpu.SemaphoreType.DMA((4,)),
            pltpu.SemaphoreType.DMA((4,)),
        ],
        compiler_params=pltpu.CompilerParams(
            collective_id=0, has_side_effects=True, vmem_limit_bytes=VMEM_BYTES
        ),
    )(
        right_sides,
        tile_scales.reshape(tiles, rank_len),
        tile_ranks.reshape(1, tiles),
        diagonal.reshape(1, cells),
        right_bases.reshape(features, cells),
        left_bases,
        near_field,
    )


def solution(mesh):
    both = ("col", "sub")
    in_specs = (
        P(None, both), P(both, None), P(None, None, both), P(None, both, None),
        P(None, both), P(both, None), P(both),
    )
    return jax.shard_map(
        functools.partial(on_device, mesh.shape["col"], mesh.shape["sub"]), mesh=mesh, in_specs=in_specs,
        out_specs=(P(None, both), P(None, both)), check_vma=False,
    )
```

```python
import functools

import jax
import jax.numpy as jnp
from jax import lax
from jax.experimental import pallas as pl
from jax.experimental.pallas import tpu as pltpu
from jax.sharding import PartitionSpec as P

MESH = pl.DeviceIdType.MESH
SHIFT = 2.0
PIVOTS = 8
VMEM_BYTES = 60 * 1024 * 1024
highest = lax.Precision.HIGHEST


def dot_rows(first, second, precision=None):
    return lax.dot_general(
        first, second, (((1,), (1,)), ((), ())),
        preferred_element_type=jnp.float32, precision=precision,
    )


def split_rows(values):
    high = values.astype(jnp.bfloat16)
    low = (values - high.astype(jnp.float32)).astype(jnp.bfloat16)
    return jnp.concatenate([high, low], axis=0)


def join_rows(product):
    half = product.shape[0] // 2
    return product[:half] + product[half:]


def kernel(
    col_count, sub_count, tiles, chunk,
    rhs_hbm, scales_hbm, ranks_hbm, diag_hbm, right_hbm, left_hbm, near_hbm,
    vectors_hbm, system_hbm,
    rhs_ref, scales_ref, ranks_ref, diag_ref, right, left, near, vectors, system_ref,
    coeff_out, coeff_in, gram_out, gram_in, gathered,
    load_sem, send_sem, recv_sem,
):
    my_col, my_sub = lax.axis_index("col"), lax.axis_index("sub")
    me = my_col * sub_count + my_sub
    chunks = right.shape[0] // chunk
    small_loads = [
        pltpu.make_async_copy(source, target, load_sem.at[chunks + 2 + n])
        for n, (source, target) in enumerate([
            (rhs_hbm, rhs_ref), (scales_hbm, scales_ref),
            (ranks_hbm, ranks_ref), (diag_hbm, diag_ref),
        ])
    ]
    right_loads = []
    for c in range(chunks):
        rows = pl.ds(c * chunk, chunk)
        right_loads.append(
            pltpu.make_async_copy(right_hbm.at[rows], right.at[rows], load_sem.at[c])
        )
    near_load = pltpu.make_async_copy(near_hbm, near, load_sem.at[chunks])
    left_load = pltpu.make_async_copy(left_hbm, left, load_sem.at[chunks + 1])
    for load in small_loads + right_loads:
        load.start()
    near_load.start()
    left_load.start()

    barrier = pltpu.get_barrier_semaphore()
    subs = [my_sub] + [lax.rem(my_sub + step, sub_count) for step in range(1, sub_count)]

    def each_partner(act):
        for sub in subs[1:]:
            act(my_col, sub)

        def column(step, carry):
            col = lax.rem(my_col + step, col_count)
            for sub in subs:
                act(col, sub)
            return carry

        lax.fori_loop(1, col_count, column, 0)

    def greet(col, sub):
        pl.semaphore_signal(barrier, inc=1, device_id=(col, sub), device_id_type=MESH)

    each_partner(greet)

    lane = lax.broadcasted_iota(jnp.int32, (8, 128), 1)
    in_first = lane < 64

    def swap(block):
        return pltpu.roll(block, 64, 1)

    for load in small_loads:
        load.wait()
    square = (tiles, tiles)
    on_diagonal = lax.broadcasted_iota(jnp.int32, square, 0) == lax.broadcasted_iota(
        jnp.int32, square, 1
    )
    ranks = jnp.sum(jnp.where(on_diagonal, ranks_ref[...], 0), axis=1, keepdims=True)
    keep = lax.broadcasted_iota(jnp.int32, scales_ref.shape, 1) < ranks
    weights = jnp.where(keep, scales_ref[...], 0.0)

    def project(stacked, phase, first):
        for c in range(chunks):
            if first:
                right_loads[c].wait()
            product = join_rows(dot_rows(stacked, right[pl.ds(c * chunk, chunk)]))
            for m in range(chunk // 128):
                i = c * (chunk // 64) + 2 * m
                pair = product[:, m * 128:(m + 1) * 128]
                pair = pair * jnp.concatenate([weights[i:i + 1], weights[i + 1:i + 2]], axis=1)
                upper, lower = pair[:8], pair[8:]
                coeff_out[phase, i] = jnp.where(in_first, upper, swap(lower))
                coeff_out[phase, i + 1] = jnp.where(in_first, swap(upper), lower)

    def remote(source, target, slot, col, sub):
        return pltpu.make_async_remote_copy(
            src_ref=source, dst_ref=target, send_sem=send_sem.at[slot], recv_sem=recv_sem.at[slot],
            device_id=(col, sub), device_id_type=MESH,
        )

    def send_coefficients(phase):
        def send(col, sub):
            other = col * sub_count + sub
            remote(coeff_out.at[phase, other], coeff_in.at[phase, me], phase, col, sub).start()

        each_partner(send)
        coeff_in[phase, me] = coeff_out[phase, me]

    def all_of(blocks, slot):
        return remote(blocks, blocks, slot, my_col, subs[1])

    def coefficients_of(phase):
        return all_of(coeff_in.at[phase, pl.ds(0, tiles - 1)], phase)

    def grams_of(which):
        return all_of(gram_in.at[which, pl.ds(0, tiles - 1)], 2 + which)

    def send_gram(which, block):
        gram_out[which] = jnp.concatenate([block[:8], block[8:]], axis=1)

        def send(col, sub):
            remote(gram_out.at[which], gram_in.at[which, me], 2 + which, col, sub).start()

        each_partner(send)
        gram_in[which, me] = gram_out[which]

    def far_field(phase):
        for m in range(tiles // 2):
            even, odd = coeff_in[phase, 2 * m], coeff_in[phase, 2 * m + 1]
            upper = jnp.where(in_first, even, swap(odd))
            lower = jnp.where(in_first, swap(even), odd)
            gathered[:, m * 128:(m + 1) * 128] = split_rows(jnp.concatenate([upper, lower], axis=0))
        return join_rows(dot_rows(gathered[...], left[...]))

    rhs = rhs_ref[...]
    diag = diag_ref[...]
    stacked = split_rows(rhs)
    project(stacked, 0, True)
    pl.semaphore_wait(barrier, tiles - 1)
    send_coefficients(0)
    near_load.wait()
    moved = (diag - SHIFT) * rhs + join_rows(dot_rows(stacked, near[...]))
    left_load.wait()
    coefficients_of(0).wait_recv()
    moved = moved + far_field(0)
    image_1 = moved + SHIFT * rhs

    count = rhs.shape[0]
    vectors[:count] = moved
    vectors[count:2 * count] = image_1
    first_store = pltpu.make_async_copy(
        vectors.at[pl.ds(0, 2 * count)], vectors_hbm.at[pl.ds(0, 2 * count)],
        load_sem.at[chunks + 6],
    )
    first_store.start()
    stacked = split_rows(moved)
    project(stacked, 1, False)
    send_coefficients(1)
    early = dot_rows(image_1, jnp.concatenate([rhs, image_1], axis=0), highest)
    send_gram(0, jnp.concatenate([early, jnp.zeros_like(early)], axis=1))
    image_2 = diag * moved + join_rows(dot_rows(stacked, near[...]))
    coefficients_of(1).wait_recv()
    image_2 = image_2 + far_field(1)

    vectors[2 * count:] = image_2
    second_store = pltpu.make_async_copy(
        vectors.at[pl.ds(2 * count, count)], vectors_hbm.at[pl.ds(2 * count, count)],
        load_sem.at[chunks + 7],
    )
    second_store.start()
    late = dot_rows(image_2, jnp.concatenate([rhs, image_1, image_2], axis=0), highest)
    cross = dot_rows(image_1, image_2, highest)
    send_gram(1, jnp.concatenate([late, cross], axis=1))

    def total(which):
        grams_of(which).wait_recv()
        summed = jnp.sum(gram_in[which], axis=0)
        return jnp.concatenate([summed, swap(summed)], axis=0)

    early, late = total(0), total(1)
    top = jnp.where(
        lax.broadcasted_iota(jnp.int32, early.shape, 1) < 32, early, pltpu.roll(late, 112, 1)
    )
    system = jnp.concatenate([top, late], axis=0)
    row_at = lax.broadcasted_iota(jnp.int32, system.shape, 0)
    for start in range(0, 32, PIVOTS):
        columns = [
            jnp.broadcast_to(system[:, 16 + k:17 + k], system.shape)
            for k in range(start, start + PIVOTS)
        ]
        for n in range(PIVOTS):
            k = start + n
            factors = columns[n]
            inverse = 1.0 / factors[k:k + 1]

            def eliminate(block):
                scaled = block[k:k + 1] * inverse
                return jnp.where(row_at == k, scaled, block - factors * scaled)

            columns[n + 1:] = [eliminate(column) for column in columns[n + 1:]]
            system = eliminate(system)
    system_ref[...] = system
    last_store = pltpu.make_async_copy(system_ref, system_hbm, load_sem.at[chunks + 8])
    last_store.start()
    coefficients_of(0).wait_send()
    coefficients_of(1).wait_send()
    grams_of(0).wait_send()
    grams_of(1).wait_send()
    first_store.wait()
    second_store.wait()
    last_store.wait()


def combine(rhs_ref, vectors_ref, system_ref, sol_ref, res_ref):
    rhs = rhs_ref[...]
    count = rhs.shape[0]
    mix = jnp.transpose(system_ref[...])[:count, :2 * count]
    basis = jnp.concatenate([rhs, vectors_ref[:count]], axis=0)
    sol_ref[...] = jnp.dot(mix, basis, precision=highest)
    res_ref[...] = rhs - jnp.dot(mix, vectors_ref[count:], precision=highest)


def on_device(
    col_count, sub_count, right_sides, left_bases, right_bases, tile_scales, tile_ranks, near_field,
    diagonal,
):
    rhs_count, cells = right_sides.shape
    tiles, rank_len, _ = right_bases.shape
    features = tiles * rank_len
    chunk = min(512, features)
    vmem = pl.BlockSpec(memory_space=pltpu.VMEM)
    anywhere = pl.BlockSpec(memory_space=pl.ANY)
    vectors, system = pl.pallas_call(
        functools.partial(kernel, col_count, sub_count, tiles, chunk),
        out_shape=[
            jax.ShapeDtypeStruct((3 * rhs_count, cells), jnp.float32),
            jax.ShapeDtypeStruct((2 * rhs_count, 128), jnp.float32),
        ],
        in_specs=[anywhere] * 7,
        out_specs=[anywhere] * 2,
        scratch_shapes=[
            pltpu.VMEM((rhs_count, cells), jnp.float32),
            pltpu.VMEM((tiles, rank_len), jnp.float32),
            pltpu.VMEM((1, tiles), jnp.int32),
            pltpu.VMEM((1, cells), jnp.float32),
            pltpu.VMEM((features, cells), jnp.bfloat16),
            pltpu.VMEM((cells, features), jnp.bfloat16),
            pltpu.VMEM((cells, cells), jnp.bfloat16),
            pltpu.VMEM((3 * rhs_count, cells), jnp.float32),
            pltpu.VMEM((2 * rhs_count, 128), jnp.float32),
            pltpu.VMEM((2, tiles, 8, 128), jnp.float32),
            pltpu.VMEM((2, tiles, 8, 128), jnp.float32),
            pltpu.VMEM((2, 8, 128), jnp.float32),
            pltpu.VMEM((2, tiles, 8, 128), jnp.float32),
            pltpu.VMEM((2 * rhs_count, features), jnp.bfloat16),
            pltpu.SemaphoreType.DMA((features // chunk + 9,)),
            pltpu.SemaphoreType.DMA((4,)),
            pltpu.SemaphoreType.DMA((4,)),
        ],
        compiler_params=pltpu.CompilerParams(
            collective_id=0, has_side_effects=True, vmem_limit_bytes=VMEM_BYTES
        ),
    )(
        right_sides,
        tile_scales.reshape(tiles, rank_len),
        tile_ranks.reshape(1, tiles),
        diagonal.reshape(1, cells),
        right_bases.reshape(features, cells),
        left_bases,
        near_field,
    )
    return pl.pallas_call(
        combine,
        out_shape=[jax.ShapeDtypeStruct((rhs_count, cells), jnp.float32)] * 2,
        in_specs=[vmem] * 3,
        out_specs=[vmem] * 2,
        compiler_params=pltpu.CompilerParams(vmem_limit_bytes=VMEM_BYTES),
    )(right_sides, vectors, system)


def solution(mesh):
    both = ("col", "sub")
    in_specs = (
        P(None, both), P(both, None), P(None, None, both), P(None, both, None),
        P(None, both), P(both, None), P(both),
    )
    return jax.shard_map(
        functools.partial(on_device, mesh.shape["col"], mesh.shape["sub"]), mesh=mesh, in_specs=in_specs,
        out_specs=(P(None, both), P(None, both)), check_vma=False,
    )
```

```python
import functools

import jax
import jax.numpy as jnp
from jax import lax
from jax.experimental import pallas as pl
from jax.experimental.pallas import tpu as pltpu
from jax.sharding import PartitionSpec as P

MESH = pl.DeviceIdType.MESH
SHIFT = 2.0
PIVOTS = 8
VMEM_BYTES = 60 * 1024 * 1024
highest = lax.Precision.HIGHEST


def dot_rows(first, second, precision=None):
    return lax.dot_general(
        first, second, (((1,), (1,)), ((), ())),
        preferred_element_type=jnp.float32, precision=precision,
    )


def split_rows(values):
    high = values.astype(jnp.bfloat16)
    low = (values - high.astype(jnp.float32)).astype(jnp.bfloat16)
    return jnp.concatenate([high, low], axis=0)


def join_rows(product):
    half = product.shape[0] // 2
    return product[:half] + product[half:]


def kernel(
    col_count, sub_count, tiles, chunk,
    rhs_hbm, scales_hbm, ranks_hbm, diag_hbm, right_hbm, left_hbm, near_hbm,
    vectors_hbm, system_hbm,
    rhs_ref, scales_ref, ranks_ref, diag_ref, right, left, near, vectors, system_ref,
    coeff_out, coeff_in, gram_out, gram_in, pair_weights,
    load_sem, send_sem, recv_sem,
):
    my_col, my_sub = lax.axis_index("col"), lax.axis_index("sub")
    me = my_col * sub_count + my_sub
    chunks = right.shape[0] // chunk
    small_loads = [
        pltpu.make_async_copy(source, target, load_sem.at[chunks + 2 + n])
        for n, (source, target) in enumerate([
            (rhs_hbm, rhs_ref), (scales_hbm, scales_ref),
            (ranks_hbm, ranks_ref), (diag_hbm, diag_ref),
        ])
    ]
    group_tiles = chunk // 64
    group_cols = group_tiles // sub_count
    my_group = my_col // group_cols
    groups = [my_group] + [lax.rem(my_group + k, chunks) for k in range(1, chunks)]
    outward = list(range(1, chunks)) + [0]

    def span(k):
        return pl.ds(pl.multiple_of(groups[k] * chunk, chunk), chunk)

    right_loads = []
    for c in outward:
        rows = span(c)
        right_loads.append(
            pltpu.make_async_copy(right_hbm.at[rows], right.at[rows], load_sem.at[c])
        )
    near_load = pltpu.make_async_copy(near_hbm, near, load_sem.at[chunks])
    left_load = pltpu.make_async_copy(left_hbm, left, load_sem.at[chunks + 1])
    for load in small_loads + right_loads:
        load.start()
    near_load.start()
    left_load.start()

    barrier = pltpu.get_barrier_semaphore()
    subs = [my_sub] + [lax.rem(my_sub + step, sub_count) for step in range(1, sub_count)]

    def each_partner(act):
        for sub in subs[1:]:
            act(my_col, sub)

        def column(step, carry):
            col = lax.rem(my_col + step, col_count)
            for sub in subs:
                act(col, sub)
            return carry

        lax.fori_loop(1, col_count, column, 0)

    def greet(col, sub):
        pl.semaphore_signal(barrier, inc=1, device_id=(col, sub), device_id_type=MESH)

    each_partner(greet)

    lane = lax.broadcasted_iota(jnp.int32, (8, 128), 1)
    in_first = lane < 64

    def swap(block):
        return pltpu.roll(block, 64, 1)

    for load in small_loads:
        load.wait()
    square = (tiles, tiles)
    on_diagonal = lax.broadcasted_iota(jnp.int32, square, 0) == lax.broadcasted_iota(
        jnp.int32, square, 1
    )
    ranks = jnp.sum(jnp.where(on_diagonal, ranks_ref[...], 0), axis=1, keepdims=True)
    keep = lax.broadcasted_iota(jnp.int32, scales_ref.shape, 1) < ranks
    weights = jnp.where(keep, scales_ref[...], 0.0)

    for m in range(tiles // 2):
        pair_weights[m:m + 1] = jnp.concatenate(
            [weights[2 * m:2 * m + 1], weights[2 * m + 1:2 * m + 2]], axis=1
        )

    def project(stacked, phase, k):
        product = join_rows(dot_rows(stacked, right[span(k)]))
        for m in range(chunk // 128):
            at = groups[k] * (group_tiles // 2) + m
            pair = product[:, m * 128:(m + 1) * 128] * pair_weights[pl.ds(at, 1)]
            upper, lower = pair[:8], pair[8:]
            coeff_out[phase, 2 * at] = jnp.where(in_first, upper, swap(lower))
            coeff_out[phase, 2 * at + 1] = jnp.where(in_first, swap(upper), lower)

    def remote(source, target, slot, col, sub, arrival=None):
        return pltpu.make_async_remote_copy(
            src_ref=source, dst_ref=target, send_sem=send_sem.at[slot],
            recv_sem=recv_sem.at[slot if arrival is None else arrival],
            device_id=(col, sub), device_id_type=MESH,
        )

    def arrival_of(phase, group):
        return 4 + phase * chunks + group

    def send_group(phase, k):
        for a in range(group_cols):
            col = groups[k] * group_cols + lax.rem(my_col + a, group_cols)
            for b, sub in enumerate(subs):
                if k == 0 and a == 0 and b == 0:
                    coeff_in[phase, me] = coeff_out[phase, me]
                    continue
                remote(
                    coeff_out.at[phase, col * sub_count + sub], coeff_in.at[phase, me], phase,
                    col, sub, arrival_of(phase, my_group),
                ).start()

    def all_of(blocks, slot):
        return remote(blocks, blocks, slot, my_col, subs[1])

    def coefficients_of(phase):
        return all_of(coeff_in.at[phase, pl.ds(0, tiles - 1)], phase)

    def grams_of(which):
        return all_of(gram_in.at[which, pl.ds(0, tiles - 1)], 2 + which)

    def send_gram(which, block):
        gram_out[which] = jnp.concatenate([block[:8], block[8:]], axis=1)

        def send(col, sub):
            remote(gram_out.at[which], gram_in.at[which, me], 2 + which, col, sub).start()

        each_partner(send)
        gram_in[which, me] = gram_out[which]

    def far_field(phase):
        total = 0.0
        for k in range(chunks):
            blocks = coeff_in.at[phase, pl.ds(0, group_tiles - (k == 0))]
            remote(
                blocks, blocks, phase, my_col, subs[1], arrival_of(phase, groups[k])
            ).wait_recv()
            pairs = []
            for m in range(group_tiles // 2):
                at = groups[k] * group_tiles + 2 * m
                even, odd = coeff_in[phase, at], coeff_in[phase, at + 1]
                upper = jnp.where(in_first, even, swap(odd))
                lower = jnp.where(in_first, swap(even), odd)
                pairs.append(split_rows(jnp.concatenate([upper, lower], axis=0)))
            total = total + join_rows(dot_rows(jnp.concatenate(pairs, axis=1), left[:, span(k)]))
        return total

    rhs = rhs_ref[...]
    diag = diag_ref[...]
    stacked = split_rows(rhs)
    for load, k in zip(right_loads, outward):
        load.wait()
        project(stacked, 0, k)
    pl.semaphore_wait(barrier, tiles - 1)
    for k in outward:
        send_group(0, k)
    near_load.wait()
    moved = (diag - SHIFT) * rhs + join_rows(dot_rows(stacked, near[...]))
    left_load.wait()
    moved = moved + far_field(0)
    image_1 = moved + SHIFT * rhs

    count = rhs.shape[0]
    vectors[:count] = moved
    vectors[count:2 * count] = image_1
    first_store = pltpu.make_async_copy(
        vectors.at[pl.ds(0, 2 * count)], vectors_hbm.at[pl.ds(0, 2 * count)],
        load_sem.at[chunks + 6],
    )
    first_store.start()
    stacked = split_rows(moved)
    for k in outward:
        project(stacked, 1, k)
        send_group(1, k)
    early = dot_rows(image_1, jnp.concatenate([rhs, image_1], axis=0), highest)
    send_gram(0, jnp.concatenate([early, jnp.zeros_like(early)], axis=1))
    image_2 = diag * moved + join_rows(dot_rows(stacked, near[...]))
    image_2 = image_2 + far_field(1)

    vectors[2 * count:] = image_2
    second_store = pltpu.make_async_copy(
        vectors.at[pl.ds(2 * count, count)], vectors_hbm.at[pl.ds(2 * count, count)],
        load_sem.at[chunks + 7],
    )
    second_store.start()
    late = dot_rows(image_2, jnp.concatenate([rhs, image_1, image_2], axis=0), highest)
    cross = dot_rows(image_1, image_2, highest)
    send_gram(1, jnp.concatenate([late, cross], axis=1))

    def total(which):
        grams_of(which).wait_recv()
        summed = jnp.sum(gram_in[which], axis=0)
        return jnp.concatenate([summed, swap(summed)], axis=0)

    early, late = total(0), total(1)
    top = jnp.where(
        lax.broadcasted_iota(jnp.int32, early.shape, 1) < 32, early, pltpu.roll(late, 112, 1)
    )
    system = jnp.concatenate([top, late], axis=0)
    row_at = lax.broadcasted_iota(jnp.int32, system.shape, 0)
    for start in range(0, 32, PIVOTS):
        columns = [
            jnp.broadcast_to(system[:, 16 + k:17 + k], system.shape)
            for k in range(start, start + PIVOTS)
        ]
        for n in range(PIVOTS):
            k = start + n
            factors = columns[n]
            inverse = 1.0 / factors[k:k + 1]

            def eliminate(block):
                scaled = block[k:k + 1] * inverse
                return jnp.where(row_at == k, scaled, block - factors * scaled)

            columns[n + 1:] = [eliminate(column) for column in columns[n + 1:]]
            system = eliminate(system)
    system_ref[...] = system
    last_store = pltpu.make_async_copy(system_ref, system_hbm, load_sem.at[chunks + 8])
    last_store.start()
    coefficients_of(0).wait_send()
    coefficients_of(1).wait_send()
    grams_of(0).wait_send()
    grams_of(1).wait_send()
    first_store.wait()
    second_store.wait()
    last_store.wait()


def combine(rhs_ref, vectors_ref, system_ref, sol_ref, res_ref):
    rhs = rhs_ref[...]
    count = rhs.shape[0]
    mix = jnp.transpose(system_ref[...])[:count, :2 * count]
    basis = jnp.concatenate([rhs, vectors_ref[:count]], axis=0)
    sol_ref[...] = jnp.dot(mix, basis, precision=highest)
    res_ref[...] = rhs - jnp.dot(mix, vectors_ref[count:], precision=highest)


def on_device(
    col_count, sub_count, right_sides, left_bases, right_bases, tile_scales, tile_ranks, near_field,
    diagonal,
):
    rhs_count, cells = right_sides.shape
    tiles, rank_len, _ = right_bases.shape
    features = tiles * rank_len
    chunk = max(features // 4, rank_len * sub_count)
    vmem = pl.BlockSpec(memory_space=pltpu.VMEM)
    anywhere = pl.BlockSpec(memory_space=pl.ANY)
    vectors, system = pl.pallas_call(
        functools.partial(kernel, col_count, sub_count, tiles, chunk),
        out_shape=[
            jax.ShapeDtypeStruct((3 * rhs_count, cells), jnp.float32),
            jax.ShapeDtypeStruct((2 * rhs_count, 128), jnp.float32),
        ],
        in_specs=[anywhere] * 7,
        out_specs=[anywhere] * 2,
        scratch_shapes=[
            pltpu.VMEM((rhs_count, cells), jnp.float32),
            pltpu.VMEM((tiles, rank_len), jnp.float32),
            pltpu.VMEM((1, tiles), jnp.int32),
            pltpu.VMEM((1, cells), jnp.float32),
            pltpu.VMEM((features, cells), jnp.bfloat16),
            pltpu.VMEM((cells, features), jnp.bfloat16),
            pltpu.VMEM((cells, cells), jnp.bfloat16),
            pltpu.VMEM((3 * rhs_count, cells), jnp.float32),
            pltpu.VMEM((2 * rhs_count, 128), jnp.float32),
            pltpu.VMEM((2, tiles, 8, 128), jnp.float32),
            pltpu.VMEM((2, tiles, 8, 128), jnp.float32),
            pltpu.VMEM((2, 8, 128), jnp.float32),
            pltpu.VMEM((2, tiles, 8, 128), jnp.float32),
            pltpu.VMEM((tiles // 2, 128), jnp.float32),
            pltpu.SemaphoreType.DMA((features // chunk + 9,)),
            pltpu.SemaphoreType.DMA((4,)),
            pltpu.SemaphoreType.DMA((4 + 2 * (features // chunk),)),
        ],
        compiler_params=pltpu.CompilerParams(
            collective_id=0, has_side_effects=True, vmem_limit_bytes=VMEM_BYTES
        ),
    )(
        right_sides,
        tile_scales.reshape(tiles, rank_len),
        tile_ranks.reshape(1, tiles),
        diagonal.reshape(1, cells),
        right_bases.reshape(features, cells),
        left_bases,
        near_field,
    )
    return pl.pallas_call(
        combine,
        out_shape=[jax.ShapeDtypeStruct((rhs_count, cells), jnp.float32)] * 2,
        in_specs=[vmem] * 3,
        out_specs=[vmem] * 2,
        compiler_params=pltpu.CompilerParams(vmem_limit_bytes=VMEM_BYTES),
    )(right_sides, vectors, system)


def solution(mesh):
    both = ("col", "sub")
    in_specs = (
        P(None, both), P(both, None), P(None, None, both), P(None, both, None),
        P(None, both), P(both, None), P(both),
    )
    return jax.shard_map(
        functools.partial(on_device, mesh.shape["col"], mesh.shape["sub"]), mesh=mesh, in_specs=in_specs,
        out_specs=(P(None, both), P(None, both)), check_vma=False,
    )
```

```python
import functools

import jax
import jax.numpy as jnp
from jax import lax
from jax.experimental import pallas as pl
from jax.experimental.pallas import tpu as pltpu
from jax.sharding import PartitionSpec as P

MESH = pl.DeviceIdType.MESH
SHIFT = 2.0
PIVOTS = 8
VMEM_BYTES = 60 * 1024 * 1024
highest = lax.Precision.HIGHEST


def dot_rows(first, second, precision=None):
    return lax.dot_general(
        first, second, (((1,), (1,)), ((), ())),
        preferred_element_type=jnp.float32, precision=precision,
    )


def split_rows(values):
    high = values.astype(jnp.bfloat16)
    low = (values - high.astype(jnp.float32)).astype(jnp.bfloat16)
    return jnp.concatenate([high, low], axis=0)


def join_rows(product):
    half = product.shape[0] // 2
    return product[:half] + product[half:]


def kernel(
    col_count, sub_count, tiles, chunk,
    rhs_hbm, scales_hbm, ranks_hbm, diag_hbm, right_hbm, left_hbm, near_hbm,
    vectors_hbm, system_hbm,
    rhs_ref, scales_ref, ranks_ref, diag_ref, right, left, near, vectors, system_ref,
    coeff_out, coeff_in, gram_out, gram_in, pair_weights,
    load_sem, send_sem, recv_sem,
):
    my_col, my_sub = lax.axis_index("col"), lax.axis_index("sub")
    me = my_col * sub_count + my_sub
    chunks = right.shape[0] // chunk
    small_loads = [
        pltpu.make_async_copy(source, target, load_sem.at[chunks + 2 + n])
        for n, (source, target) in enumerate([
            (rhs_hbm, rhs_ref), (scales_hbm, scales_ref),
            (ranks_hbm, ranks_ref), (diag_hbm, diag_ref),
        ])
    ]
    group_tiles = chunk // 64
    group_cols = group_tiles // sub_count
    my_group = my_col // group_cols
    groups = [my_group] + [lax.rem(my_group + k, chunks) for k in range(1, chunks)]
    outward = list(range(1, chunks)) + [0]

    def span(k):
        return pl.ds(pl.multiple_of(groups[k] * chunk, chunk), chunk)

    right_loads = []
    for c in outward:
        rows = span(c)
        right_loads.append(
            pltpu.make_async_copy(right_hbm.at[rows], right.at[rows], load_sem.at[c])
        )
    near_load = pltpu.make_async_copy(near_hbm, near, load_sem.at[chunks])
    left_load = pltpu.make_async_copy(left_hbm, left, load_sem.at[chunks + 1])
    for load in small_loads + right_loads:
        load.start()
    near_load.start()
    left_load.start()

    barrier = pltpu.get_barrier_semaphore()
    subs = [my_sub] + [lax.rem(my_sub + step, sub_count) for step in range(1, sub_count)]

    def each_partner(act):
        for sub in subs[1:]:
            act(my_col, sub)

        def column(step, carry):
            col = lax.rem(my_col + step, col_count)
            for sub in subs:
                act(col, sub)
            return carry

        lax.fori_loop(1, col_count, column, 0)

    def greet(col, sub):
        pl.semaphore_signal(barrier, inc=1, device_id=(col, sub), device_id_type=MESH)

    each_partner(greet)

    lane = lax.broadcasted_iota(jnp.int32, (8, 128), 1)
    in_first = lane < 64

    def swap(block):
        return pltpu.roll(block, 64, 1)

    for load in small_loads:
        load.wait()
    square = (tiles, tiles)
    on_diagonal = lax.broadcasted_iota(jnp.int32, square, 0) == lax.broadcasted_iota(
        jnp.int32, square, 1
    )
    ranks = jnp.sum(jnp.where(on_diagonal, ranks_ref[...], 0), axis=1, keepdims=True)
    keep = lax.broadcasted_iota(jnp.int32, scales_ref.shape, 1) < ranks
    weights = jnp.where(keep, scales_ref[...], 0.0)

    for m in range(tiles // 2):
        pair_weights[m:m + 1] = jnp.concatenate(
            [weights[2 * m:2 * m + 1], weights[2 * m + 1:2 * m + 2]], axis=1
        )

    def project(stacked, phase, k):
        product = join_rows(dot_rows(stacked, right[span(k)]))
        for m in range(chunk // 128):
            at = groups[k] * (group_tiles // 2) + m
            pair = product[:, m * 128:(m + 1) * 128] * pair_weights[pl.ds(at, 1)]
            upper, lower = pair[:8], pair[8:]
            coeff_out[phase, 2 * at] = jnp.where(in_first, upper, swap(lower))
            coeff_out[phase, 2 * at + 1] = jnp.where(in_first, swap(upper), lower)

    def remote(source, target, slot, col, sub, arrival=None):
        return pltpu.make_async_remote_copy(
            src_ref=source, dst_ref=target, send_sem=send_sem.at[slot],
            recv_sem=recv_sem.at[slot if arrival is None else arrival],
            device_id=(col, sub), device_id_type=MESH,
        )

    def arrival_of(phase, group):
        return 4 + phase * chunks + group

    def send_group(phase, k):
        for a in range(group_cols):
            col = groups[k] * group_cols + lax.rem(my_col + a, group_cols)
            for b, sub in enumerate(subs):
                if k == 0 and a == 0 and b == 0:
                    coeff_in[phase, me] = coeff_out[phase, me]
                    continue
                remote(
                    coeff_out.at[phase, col * sub_count + sub], coeff_in.at[phase, me], phase,
                    col, sub, arrival_of(phase, my_group),
                ).start()

    def all_of(blocks, slot):
        return remote(blocks, blocks, slot, my_col, subs[1])

    def coefficients_of(phase):
        return all_of(coeff_in.at[phase, pl.ds(0, tiles - 1)], phase)

    def grams_of(which):
        return all_of(gram_in.at[which, pl.ds(0, tiles - 1)], 2 + which)

    def send_gram(which, block):
        gram_out[which] = jnp.concatenate([block[:8], block[8:]], axis=1)

        def send(col, sub):
            remote(gram_out.at[which], gram_in.at[which, me], 2 + which, col, sub).start()

        each_partner(send)
        gram_in[which, me] = gram_out[which]

    def far_field(phase):
        total = 0.0
        for k in range(chunks):
            blocks = coeff_in.at[phase, pl.ds(0, group_tiles - (k == 0))]
            remote(
                blocks, blocks, phase, my_col, subs[1], arrival_of(phase, groups[k])
            ).wait_recv()
            pairs = []
            for m in range(group_tiles // 2):
                at = groups[k] * group_tiles + 2 * m
                even, odd = coeff_in[phase, at], coeff_in[phase, at + 1]
                upper = jnp.where(in_first, even, swap(odd))
                lower = jnp.where(in_first, swap(even), odd)
                pairs.append(split_rows(jnp.concatenate([upper, lower], axis=0)))
            total = total + join_rows(dot_rows(jnp.concatenate(pairs, axis=1), left[:, span(k)]))
        return total

    rhs = rhs_ref[...]
    diag = diag_ref[...]
    stacked = split_rows(rhs)
    for load, k in zip(right_loads, outward):
        load.wait()
        if k == 0:
            pl.semaphore_wait(barrier, tiles - 1)
            for sent in outward[:-1]:
                send_group(0, sent)
        project(stacked, 0, k)
    send_group(0, 0)
    near_load.wait()
    moved = (diag - SHIFT) * rhs + join_rows(dot_rows(stacked, near[...]))
    left_load.wait()
    moved = moved + far_field(0)
    image_1 = moved + SHIFT * rhs

    count = rhs.shape[0]
    vectors[:count] = moved
    vectors[count:2 * count] = image_1
    first_store = pltpu.make_async_copy(
        vectors.at[pl.ds(0, 2 * count)], vectors_hbm.at[pl.ds(0, 2 * count)],
        load_sem.at[chunks + 6],
    )
    first_store.start()
    stacked = split_rows(moved)
    for k in outward:
        project(stacked, 1, k)
        send_group(1, k)
    early = dot_rows(image_1, jnp.concatenate([rhs, image_1], axis=0), highest)
    send_gram(0, jnp.concatenate([early, jnp.zeros_like(early)], axis=1))
    image_2 = diag * moved + join_rows(dot_rows(stacked, near[...]))
    image_2 = image_2 + far_field(1)

    vectors[2 * count:] = image_2
    second_store = pltpu.make_async_copy(
        vectors.at[pl.ds(2 * count, count)], vectors_hbm.at[pl.ds(2 * count, count)],
        load_sem.at[chunks + 7],
    )
    second_store.start()
    late = dot_rows(image_2, jnp.concatenate([rhs, image_1, image_2], axis=0), highest)
    cross = dot_rows(image_1, image_2, highest)
    send_gram(1, jnp.concatenate([late, cross], axis=1))

    def total(which):
        grams_of(which).wait_recv()
        summed = jnp.sum(gram_in[which], axis=0)
        return jnp.concatenate([summed, swap(summed)], axis=0)

    early, late = total(0), total(1)
    top = jnp.where(
        lax.broadcasted_iota(jnp.int32, early.shape, 1) < 32, early, pltpu.roll(late, 112, 1)
    )
    system = jnp.concatenate([top, late], axis=0)
    row_at = lax.broadcasted_iota(jnp.int32, system.shape, 0)
    for start in range(0, 32, PIVOTS):
        columns = [
            jnp.broadcast_to(system[:, 16 + k:17 + k], system.shape)
            for k in range(start, start + PIVOTS)
        ]
        for n in range(PIVOTS):
            k = start + n
            factors = columns[n]
            inverse = 1.0 / factors[k:k + 1]

            def eliminate(block):
                scaled = block[k:k + 1] * inverse
                return jnp.where(row_at == k, scaled, block - factors * scaled)

            columns[n + 1:] = [eliminate(column) for column in columns[n + 1:]]
            system = eliminate(system)
    system_ref[...] = system
    last_store = pltpu.make_async_copy(system_ref, system_hbm, load_sem.at[chunks + 8])
    last_store.start()
    coefficients_of(0).wait_send()
    coefficients_of(1).wait_send()
    grams_of(0).wait_send()
    grams_of(1).wait_send()
    first_store.wait()
    second_store.wait()
    last_store.wait()


def combine(rhs_ref, vectors_ref, system_ref, sol_ref, res_ref):
    rhs = rhs_ref[...]
    count = rhs.shape[0]
    mix = jnp.transpose(system_ref[...])[:count, :2 * count]
    basis = jnp.concatenate([rhs, vectors_ref[:count]], axis=0)
    sol_ref[...] = jnp.dot(mix, basis, precision=highest)
    res_ref[...] = rhs - jnp.dot(mix, vectors_ref[count:], precision=highest)


def on_device(
    col_count, sub_count, right_sides, left_bases, right_bases, tile_scales, tile_ranks, near_field,
    diagonal,
):
    rhs_count, cells = right_sides.shape
    tiles, rank_len, _ = right_bases.shape
    features = tiles * rank_len
    chunk = max(features // 4, rank_len * sub_count)
    vmem = pl.BlockSpec(memory_space=pltpu.VMEM)
    anywhere = pl.BlockSpec(memory_space=pl.ANY)
    vectors, system = pl.pallas_call(
        functools.partial(kernel, col_count, sub_count, tiles, chunk),
        out_shape=[
            jax.ShapeDtypeStruct((3 * rhs_count, cells), jnp.float32),
            jax.ShapeDtypeStruct((2 * rhs_count, 128), jnp.float32),
        ],
        in_specs=[anywhere] * 7,
        out_specs=[anywhere] * 2,
        scratch_shapes=[
            pltpu.VMEM((rhs_count, cells), jnp.float32),
            pltpu.VMEM((tiles, rank_len), jnp.float32),
            pltpu.VMEM((1, tiles), jnp.int32),
            pltpu.VMEM((1, cells), jnp.float32),
            pltpu.VMEM((features, cells), jnp.bfloat16),
            pltpu.VMEM((cells, features), jnp.bfloat16),
            pltpu.VMEM((cells, cells), jnp.bfloat16),
            pltpu.VMEM((3 * rhs_count, cells), jnp.float32),
            pltpu.VMEM((2 * rhs_count, 128), jnp.float32),
            pltpu.VMEM((2, tiles, 8, 128), jnp.float32),
            pltpu.VMEM((2, tiles, 8, 128), jnp.float32),
            pltpu.VMEM((2, 8, 128), jnp.float32),
            pltpu.VMEM((2, tiles, 8, 128), jnp.float32),
            pltpu.VMEM((tiles // 2, 128), jnp.float32),
            pltpu.SemaphoreType.DMA((features // chunk + 9,)),
            pltpu.SemaphoreType.DMA((4,)),
            pltpu.SemaphoreType.DMA((4 + 2 * (features // chunk),)),
        ],
        compiler_params=pltpu.CompilerParams(
            collective_id=0, has_side_effects=True, vmem_limit_bytes=VMEM_BYTES
        ),
    )(
        right_sides,
        tile_scales.reshape(tiles, rank_len),
        tile_ranks.reshape(1, tiles),
        diagonal.reshape(1, cells),
        right_bases.reshape(features, cells),
        left_bases,
        near_field,
    )
    return pl.pallas_call(
        combine,
        out_shape=[jax.ShapeDtypeStruct((rhs_count, cells), jnp.float32)] * 2,
        in_specs=[vmem] * 3,
        out_specs=[vmem] * 2,
        compiler_params=pltpu.CompilerParams(vmem_limit_bytes=VMEM_BYTES),
    )(right_sides, vectors, system)


def solution(mesh):
    both = ("col", "sub")
    in_specs = (
        P(None, both), P(both, None), P(None, None, both), P(None, both, None),
        P(None, both), P(both, None), P(both),
    )
    return jax.shard_map(
        functools.partial(on_device, mesh.shape["col"], mesh.shape["sub"]), mesh=mesh, in_specs=in_specs,
        out_specs=(P(None, both), P(None, both)), check_vma=False,
    )
```
